512 devices in a mesh: play: 64 (over y_lo, z, core), col: 8 (over y_hi, x).
Axes of the slice: x: 4, y: 8 (y_hi: 2, y_lo: 4; y = y_hi * 4 + y_lo), z: 8, core: 2. Of those that a mesh axis runs over, the one named last changes fastest.
Arguments:
- embeddings: bfloat16 [65536, 1024], P('play', 'col'), may hold values from -1 to 1
- labels: int32 [3, 65536], P(None, 'play'), may hold values from 0 to 1023
Outputs:
- gradient: float32 [65536, 1024], P('play', 'col')
The draws below stay inside these ranges and needn't reach their ends.
All inputs are finite; a program needn't handle non-finite values.
Results may differ from the reference program's by a relative error of at most 0.0014.
Values may be sent and summed in bfloat16 or wider, within the bound.
A program may use at most 64 MiB of HBM per device.

```python
import jax
import jax.numpy as jnp
from jax import lax

D = 1024
B = 1024
ROUNDS = 3
ITEMS = 65536


def place_ends(array, own_key, least, high):
    longest = array.shape.index(max(array.shape))
    spots = []
    for shift in (0, 1):
        where = [jax.random.randint(jax.random.fold_in(own_key, axis), (), 0, length) for axis, length in enumerate(array.shape)]
        where[longest] = (where[longest] + shift) % array.shape[longest]
        spots.append(tuple(where))
    return array.at[spots[0]].set(least).at[spots[1]].set(high)


def block_scale(own_key, dims, shards, least, top_value):
    def one(dim, shards_of):
        draws = jax.random.uniform(jax.random.fold_in(jax.random.fold_in(own_key, 6), dim), (shards_of,), jnp.float32, least / len(shards), top_value / len(shards))
        return jnp.repeat(jnp.exp(draws), dims[dim] // shards_of).reshape((-1,) + (1,) * (len(dims) - dim - 1))

    loudness = one(*shards[0])
    for cut in shards[1:]:
        loudness = loudness * one(*cut)
    return loudness


def gaussian(key, dims, width, most, cuts=(), held_as=jnp.bfloat16):
    array = jax.random.normal(key, dims, jnp.float32) * width
    if len(cuts) > 0:
        array = block_scale(key, dims, cuts, -0.22, 0.18) * array
    return jnp.clip(array, min=-most, max=most).astype(held_as)


def setup_inputs(seed: int = 0) -> dict:
    key_of = jax.random.split(jax.random.key(seed), 3)
    return {
        "embeddings": gaussian(key_of[0], (ITEMS, D), 0.18, 1.0, ((0, 64), (1, 8))),
        "labels": place_ends(jax.random.randint(key_of[1], (ROUNDS, ITEMS), 0, B), jax.random.fold_in(key_of[1], 1), 0, B - 1).astype(jnp.int32),
    }


scale_logit = 2.0
bias_logit = -1.0
loss_scale = 0.125


def reference(embeddings, labels):
    players = embeddings.shape[0] // B
    blocks = embeddings.reshape(players, B, D)
    gradient = jnp.zeros((players, B, D), jnp.float32)
    for round_idx in range(ROUNDS):
        partners = jnp.roll(blocks, round_idx + 1, axis=0)
        label_rows = labels[round_idx].reshape(players, B)

        def one_pair(items):
            own_rows, other_rows, positive = items
            scores = lax.dot_general(own_rows, other_rows, (((1,), (1,)), ((), ())), preferred_element_type=jnp.float32)
            target = (positive[:, None] == jnp.arange(B, dtype=jnp.int32)[None, :]).astype(jnp.float32)
            slope = (loss_scale * scale_logit * (jax.nn.sigmoid(scale_logit * scores + bias_logit) - target)).astype(jnp.bfloat16)
            own_part = jnp.dot(slope, other_rows, preferred_element_type=jnp.float32)
            other_part = lax.dot_general(slope, own_rows, (((0,), (0,)), ((), ())), preferred_element_type=jnp.float32)
            return own_part, other_part

        own_terms, other_terms = lax.map(one_pair, (blocks, partners, label_rows))
        gradient = gradient + own_terms + jnp.roll(other_terms, -(round_idx + 1), axis=0)
    return gradient.reshape(players * B, D)
```

```python
import jax
import jax.numpy as jnp
from jax import lax
from jax.experimental import pallas as pl
from jax.experimental.pallas import tpu as pltpu
from jax.sharding import PartitionSpec as P

MESH = pl.DeviceIdType.MESH
OWN = 3
SLOTS = (0, 1, 2, 4, 5, 6)
ROUNDS = 3


def kernel(
    e_ref, lab_ref, out_ref,
    far, q_ref, own, slope, lab_rows, lab_cols, lab_in,
    part, via, last,
    send_sem, local_sem, r_far, r_qa, r_qb, r_own, r_z, r_lab, r_via, r_last, r_out,
):
    play, col = lax.axis_index("play"), lax.axis_index("col")
    x, h = lax.rem(col, 4), col // 4
    c = lax.rem(play, 2)
    line = h * 64 + play

    def along(delta):
        to = lax.rem(line + delta + 128, 128)
        return {"play": lax.rem(to, 64), "col": (to // 64) * 4 + x}

    def beside(delta):
        return {"play": play, "col": h * 4 + lax.rem(x + delta, 4)}

    def half_of(delta):
        return lax.rem(line + delta + 128, 128) // 64

    across = {"play": play, "col": (1 - h) * 4 + x}
    twin = {"play": play + 1 - 2 * c, "col": col}

    barrier = pltpu.get_barrier_semaphore()
    greeted = [along(d) for d in (-3, -2, -1, 1, 2, 3)] + [beside(o) for o in (1, 2, 3)] + [across]
    for device in greeted:
        pl.semaphore_signal(barrier, inc=1, device_id=device, device_id_type=MESH)
    pl.semaphore_wait(barrier, len(greeted))

    sent = []

    def send(src, dst, recv, device):
        copy = pltpu.make_async_remote_copy(
            src_ref=src, dst_ref=dst, send_sem=send_sem.at[len(sent)], recv_sem=recv,
            device_id=device, device_id_type=MESH,
        )
        copy.start()
        sent.append(copy)

    def arrived(dst, recv):
        pltpu.make_async_copy(dst, dst, recv).wait()

    def place(src, dst, index):
        copy = pltpu.make_async_copy(src, dst, local_sem.at[index])
        copy.start()
        return copy

    for j in range(2):
        send(e_ref.at[:, j], far.at[:, j], r_far.at[j], across)
    for o in (2, 1, 3):
        send(e_ref.at[lax.rem(x + o, 4)], q_ref.at[OWN, h, x], r_qa.at[x], beside(o))
    mine_a = place(e_ref.at[x], q_ref.at[OWN, h, x], 0)
    for d in (1, 2, 3):
        send(lab_ref, lab_in.at[d - 1], r_lab.at[d - 1], along(-d))
    for o in (2, 1, 3):
        send(e_ref.at[pl.ds(2 * h, 2)], own.at[h, x], r_own.at[h, x], beside(o))
    own_a = place(e_ref.at[pl.ds(2 * h, 2)], own.at[h, x], 1)

    lab = lab_ref[:, pl.ds(pl.multiple_of(h * 512, 512), 512)]
    lab = jnp.concatenate([lab, jnp.zeros((8 - ROUNDS, 512), jnp.int32)], axis=0).T
    for r in range(ROUNDS):
        lab_rows[r] = jnp.broadcast_to(lab[:, r : r + 1], (512, 128))
    lab_rows[ROUNDS] = lax.broadcasted_iota(jnp.int32, (512, 128), 0) + h * 512
    lab_cols[ROUNDS] = lax.broadcasted_iota(jnp.int32, (8, 256), 1) + x * 256

    def piece(slot, half, index):
        if index == 0:
            return q_ref.at[slot, half]
        return q_ref.at[slot, 1 - half, :, index - 1]

    def spread(index):
        src = piece(OWN, h, index)
        send(src, piece(1, h, index), r_z.at[1, index], along(2))
        send(src, piece(5, h, index), r_z.at[5, index], along(-2))
        slot = 2 + 2 * c
        send(src, piece(slot, h, index), r_z.at[slot, index], twin)

    def relay(index):
        below, above = half_of(-2), half_of(2)
        arrived(piece(1, below, index), r_z.at[1, index])
        arrived(piece(5, above, index), r_z.at[5, index])
        half = jnp.where(c == 1, below, above)
        src, dst = 5 - 4 * c, 6 - 6 * c
        send(piece(src, half, index), piece(dst, half, index), r_z.at[dst, index], along(2 * c - 1))
        dst = 2 * c
        send(piece(1, below, index), piece(dst, below, index), r_z.at[dst, index], twin)
        dst = 4 + 2 * c
        send(piece(5, above, index), piece(dst, above, index), r_z.at[dst, index], twin)

    def quarter(j):
        arrived(far.at[:, j], r_far.at[j])
        for o in (2, 1, 3):
            send(far.at[lax.rem(x + o, 4), j], q_ref.at[OWN, 1 - h, x, j], r_qb.at[x, j], beside(o))
        return place(far.at[x, j], q_ref.at[OWN, 1 - h, x, j], 2 + j)

    def quarter_arrived(j):
        for o in (1, 2, 3):
            peer = lax.rem(x + o, 4)
            arrived(q_ref.at[OWN, 1 - h, peer, j], r_qb.at[peer, j])

    for o in (1, 2, 3):
        peer = lax.rem(x + o, 4)
        arrived(q_ref.at[OWN, h, peer], r_qa.at[peer])
    mine_a.wait()
    spread(0)
    mine_b = quarter(0)
    quarter_arrived(0)
    mine_b.wait()
    spread(1)
    mine_b = quarter(1)
    for o in (2, 1, 3):
        send(far.at[pl.ds(2 * h, 2)], own.at[1 - h, x], r_own.at[1 - h, x], beside(o))
    own_b = place(far.at[pl.ds(2 * h, 2)], own.at[1 - h, x], 4)
    relay(0)
    quarter_arrived(1)
    mine_b.wait()
    spread(2)
    relay(1)
    for d in (1, 2, 3):
        arrived(lab_in.at[d - 1], r_lab.at[d - 1])
        row = lab_in[d - 1, d - 1 : d, pl.ds(pl.multiple_of(x * 256, 256), 256)]
        lab_cols[d - 1] = jnp.broadcast_to(row, (8, 256))
    own_a.wait()
    own_b.wait()
    for o in (1, 2, 3):
        peer = lax.rem(x + o, 4)
        for half in range(2):
            arrived(own.at[half, peer], r_own.at[half, peer])

    def wide(ref, *at):
        return jnp.concatenate(
            [ref[(*at, half, k)].reshape(-1, 128) for half in range(2) for k in range(4)], axis=1
        )

    def pair(slot):
        scores = lax.dot_general(
            wide(own), wide(q_ref, slot), (((1,), (1,)), ((), ())), preferred_element_type=jnp.float32
        )
        below = slot < OWN
        rows = lab_rows[jnp.where(below, OWN - 1 - slot, ROUNDS)]
        cols = lab_cols[jnp.where(below, ROUNDS, slot - OWN - 1)][:1]
        hit = jnp.concatenate([rows, rows], axis=1) == cols
        base = jnp.where(hit, -0.125, 0.125)
        slope[slot] = (0.125 * jnp.tanh(scores - 0.5) + base).astype(jnp.bfloat16)

    def slot_arrived(slot, delta, indices=(0, 1, 2)):
        for index in indices:
            arrived(piece(slot, half_of(delta), index), r_z.at[slot, index])

    def step(i, _):
        slot = jnp.where(i == 0, 4 - 2 * c, 0)
        slot = jnp.where(i == 1, 1, slot)
        slot = jnp.where(i == 2, 5, slot)
        slot = jnp.where(i == 3, 2 - 2 * c, slot)
        slot = jnp.where(i == 4, 6 - 2 * c, slot)
        slot = jnp.where(i == 5, 6 * c, slot)

        @pl.when((i == 0) | (i > 2))
        def _():
            slot_arrived(slot, slot - OWN)

        pair(slot)
        return 0

    relay(2)
    lax.fori_loop(0, 6, step, 0)

    def product(o):
        xd = lax.rem(x + o, 4)
        left = jnp.concatenate([slope[s] for s in SLOTS], axis=1)
        right = jnp.concatenate(
            [
                jnp.concatenate([q_ref[s, half, xd].reshape(256, 128) for half in range(2)], axis=1)
                for s in SLOTS
            ],
            axis=0,
        )
        value = jnp.dot(left, right, preferred_element_type=jnp.float32)
        for half in range(2):
            part[o, half] = value[:, half * 128 : half * 128 + 128].reshape(2, 2, 128, 128)

    product(2)
    for j in range(2):
        send(part.at[2, :, 0, j], via.at[0, j], r_via.at[0, j], beside(1))
        send(part.at[2, :, 1, j], via.at[1, j], r_via.at[1, j], beside(3))
    product(1)
    for j in range(2):
        send(part.at[1, :, 1, j], last.at[0, :, 1, j], r_last.at[0, 1, j], beside(1))
    product(3)
    for j in range(2):
        send(part.at[3, :, 0, j], last.at[1, :, 0, j], r_last.at[1, 0, j], beside(3))
    for j in range(2):
        arrived(via.at[0, j], r_via.at[0, j])
        part[1, :, 0, j] += via[0, j]
        send(part.at[1, :, 0, j], last.at[0, :, 0, j], r_last.at[0, 0, j], beside(1))
        arrived(via.at[1, j], r_via.at[1, j])
        part[3, :, 1, j] += via[1, j]
        send(part.at[3, :, 1, j], last.at[1, :, 1, j], r_last.at[1, 1, j], beside(3))
    product(0)
    for j in range(2):
        for side in range(2):
            arrived(last.at[0, :, side, j], r_last.at[0, side, j])
            arrived(last.at[1, :, side, j], r_last.at[1, side, j])
            part[0, 1 - h, side, j] += last[0, 1 - h, side, j] + last[1, 1 - h, side, j]
            send(part.at[0, 1 - h, side, j], out_ref.at[2 * h + side, j], r_out.at[side, j], across)
            out_ref[2 * h + side, j] = part[0, h, side, j] + last[0, h, side, j] + last[1, h, side, j]
    for j in range(2):
        for side in range(2):
            arrived(out_ref.at[2 * (1 - h) + side, j], r_out.at[side, j])
    for copy in sent:
        copy.wait_send()


def shards(embeddings, labels):
    bf16, f32, dma = jnp.bfloat16, jnp.float32, pltpu.SemaphoreType.DMA
    out = pl.pallas_call(
        kernel,
        out_shape=jax.ShapeDtypeStruct((4, 2, 128, 128), f32),
        in_specs=[pl.BlockSpec(memory_space=pltpu.VMEM)] * 2,
        out_specs=pl.BlockSpec(memory_space=pltpu.VMEM),
        scratch_shapes=[
            pltpu.VMEM((4, 2, 128, 128), bf16),
            pltpu.VMEM((7, 2, 4, 2, 128, 128), bf16),
            pltpu.VMEM((2, 4, 2, 2, 128, 128), bf16),
            pltpu.VMEM((7, 512, 256), bf16),
            pltpu.VMEM((ROUNDS + 1, 512, 128), jnp.int32),
            pltpu.VMEM((ROUNDS + 1, 8, 256), jnp.int32),
            pltpu.VMEM((ROUNDS, ROUNDS, 1024), jnp.int32),
            pltpu.VMEM((4, 2, 2, 2, 128, 128), f32),
            pltpu.VMEM((2, 2, 2, 128, 128), f32),
            pltpu.VMEM((2, 2, 2, 2, 128, 128), f32),
            dma((64,)), dma((5,)), dma((2,)), dma((4,)), dma((4, 2)), dma((2, 4)), dma((7, 3)),
            dma((3,)), dma((2, 2)), dma((2, 2, 2)), dma((2, 2)),
        ],
        compiler_params=pltpu.CompilerParams(
            collective_id=0, has_side_effects=True, vmem_limit_bytes=40 * 2**20
        ),
    )(embeddings.reshape(4, 2, 128, 128), labels)
    return out.reshape(1024, 128)


def solution(mesh):
    return jax.shard_map(
        shards,
        mesh=mesh,
        in_specs=(P("play", "col"), P(None, "play")),
        out_specs=P("play", "col"),
        check_vma=False,
    )
```

```python
import jax
import jax.numpy as jnp
from jax import lax
from jax.experimental import pallas as pl
from jax.experimental.pallas import tpu as pltpu
from jax.sharding import PartitionSpec as P

MESH = pl.DeviceIdType.MESH
OWN = 3
SLOTS = (0, 1, 2, 4, 5, 6)
ROUNDS = 3
PARTS = 4
ROWS = 256 // PARTS
FULL = (1, 3)


def kernel(
    e_hbm, lab_hbm, out_ref,
    e_ref, lab_ref, far, hop, q_ref, own, slope, lab_rows, lab_cols, lab_in,
    part, small, got, got_small,
    send_sem, local_sem, r_far, r_qa, r_qb, r_own, r_ob, r_z, r_hop, r_lab, r_got, r_small, r_out,
):
    play, col = lax.axis_index("play"), lax.axis_index("col")
    x, h = lax.rem(col, 4), col // 4
    c = lax.rem(play, 2)
    line = h * 64 + play

    def along(delta):
        to = lax.rem(line + delta + 128, 128)
        return {"play": lax.rem(to, 64), "col": (to // 64) * 4 + x}

    def beside(delta):
        return {"play": play, "col": h * 4 + lax.rem(x + delta, 4)}

    def half_of(delta):
        return lax.rem(line + delta + 128, 128) // 64

    across = {"play": play, "col": (1 - h) * 4 + x}
    twin = {"play": play + 1 - 2 * c, "col": col}

    barrier = pltpu.get_barrier_semaphore()
    greeted = [along(d) for d in (-3, -2, -1, 1, 2, 3)] + [beside(o) for o in (1, 2, 3)] + [across]
    for device in greeted:
        pl.semaphore_signal(barrier, inc=1, device_id=device, device_id_type=MESH)

    z = lax.rem(play // 2, 8)
    edge = (z == 0) | (z == 7)
    other_end = along(jnp.where(z == 0, 14, -14))
    onward = jnp.where(z == 0, 16, -16)

    @pl.when(edge)
    def _():
        for device in (other_end, along(16), along(-16)):
            pl.semaphore_signal(barrier, inc=1, device_id=device, device_id_type=MESH)

    sent = []

    def send(src, dst, recv, device):
        copy = pltpu.make_async_remote_copy(
            src_ref=src, dst_ref=dst, send_sem=send_sem.at[len(sent)], recv_sem=recv,
            device_id=device, device_id_type=MESH,
        )
        copy.start()
        sent.append(copy)

    def arrived(dst, recv):
        pltpu.make_async_copy(dst, dst, recv).wait()

    def place(src, dst, index):
        copy = pltpu.make_async_copy(src, dst, local_sem.at[index])
        copy.start()
        return copy

    fetch_lab = place(lab_hbm, lab_ref, 0)
    fetch_e = place(e_hbm, e_ref, 1)
    fetch_lab.wait()

    lab = lab_ref[:, pl.ds(pl.multiple_of(h * 512, 512), 512)]
    lab = jnp.concatenate([lab, jnp.zeros((8 - ROUNDS, 512), jnp.int32)], axis=0).T
    for r in range(ROUNDS):
        lab_rows[r] = jnp.broadcast_to(lab[:, r : r + 1], (512, 128))
    lab_rows[ROUNDS] = lax.broadcasted_iota(jnp.int32, (512, 128), 0) + h * 512
    lab_cols[ROUNDS] = lax.broadcasted_iota(jnp.int32, (8, 256), 1) + x * 256
    fetch_e.wait()
    pl.semaphore_wait(barrier, jnp.where(edge, len(greeted) + 3, len(greeted)))

    for j in range(PARTS):
        send(e_ref.at[:, j], far.at[:, j], r_far.at[j], across)
    for o in (2, 1, 3):
        send(e_ref.at[lax.rem(x + o, 4)], q_ref.at[OWN, h, x], r_qa.at[x], beside(o))
    mine_a = place(e_ref.at[x], q_ref.at[OWN, h, x], 0)
    for d in (1, 2, 3):
        send(lab_ref, lab_in.at[d - 1], r_lab.at[d - 1], along(-d))
    for o in (2, 1, 3):
        send(e_ref.at[pl.ds(2 * h, 2)], own.at[h, x], r_own.at[x], beside(o))
    own_a = place(e_ref.at[pl.ds(2 * h, 2)], own.at[h, x], 1)

    def piece(slot, half, index):
        if index == 0:
            return q_ref.at[slot, half]
        return q_ref.at[slot, 1 - half, :, index - 1]

    def leave(way):
        slot = jnp.where(z == 0, 1, 5)
        src, dst, recv, device = (
            (piece(OWN, h, 0), piece(1, h, 0), r_z.at[1, 0], along(2)),
            (piece(OWN, h, 0), piece(5, h, 0), r_z.at[5, 0], along(-2)),
            (piece(OWN, h, 0), hop, r_hop.at[0], other_end),
            (hop, piece(slot, h, 0), r_z.at[slot, 0], along(onward)),
        )[way]
        return pltpu.make_async_remote_copy(
            src_ref=src, dst_ref=dst, send_sem=send_sem.at[124 + way], recv_sem=recv,
            device_id=device, device_id_type=MESH,
        )

    def spread(index):
        src = piece(OWN, h, index)
        if index == 0:
            for copy, inside in (leave(0), z != 7), (leave(1), z != 0), (leave(2), edge):
                pl.when(inside)(copy.start)
        else:
            send(src, piece(1, h, index), r_z.at[1, index], along(2))
            send(src, piece(5, h, index), r_z.at[5, index], along(-2))
        slot = 2 + 2 * c
        send(src, piece(slot, h, index), r_z.at[slot, index], twin)

    def relay(index):
        below, above = half_of(-2), half_of(2)
        arrived(piece(1, below, index), r_z.at[1, index])
        arrived(piece(5, above, index), r_z.at[5, index])
        half = jnp.where(c == 1, below, above)
        src, dst = 5 - 4 * c, 6 - 6 * c
        send(piece(src, half, index), piece(dst, half, index), r_z.at[dst, index], along(2 * c - 1))
        dst = 2 * c
        send(piece(1, below, index), piece(dst, below, index), r_z.at[dst, index], twin)
        dst = 4 + 2 * c
        send(piece(5, above, index), piece(dst, above, index), r_z.at[dst, index], twin)

    def fan(j):
        arrived(far.at[:, j], r_far.at[j])
        for o in (2, 1, 3):
            send(far.at[lax.rem(x + o, 4), j], q_ref.at[OWN, 1 - h, x, j], r_qb.at[x, j], beside(o))
        place(far.at[x, j], q_ref.at[OWN, 1 - h, x, j], 2 + j)

    def fan_arrived(j):
        for o in (1, 2, 3):
            peer = lax.rem(x + o, 4)
            arrived(q_ref.at[OWN, 1 - h, peer, j], r_qb.at[peer, j])
        pltpu.make_async_copy(far.at[x, j], q_ref.at[OWN, 1 - h, x, j], local_sem.at[2 + j]).wait()

    for o in (1, 2, 3):
        peer = lax.rem(x + o, 4)
        arrived(q_ref.at[OWN, h, peer], r_qa.at[peer])
    mine_a.wait()
    spread(0)
    fan(0)

    fan(1)
    fan_arrived(0)
    spread(1)
    @pl.when(edge)
    def _():
        leave(2).wait_recv()
        leave(3).start()

    fan(2)
    fan_arrived(1)
    spread(2)
    fan(3)
    for o in (2, 1, 3):
        send(far.at[pl.ds(2 * h, 2)], own.at[1 - h, x], r_ob.at[x], beside(o))
    own_b = place(far.at[pl.ds(2 * h, 2)], own.at[1 - h, x], 2 + PARTS)
    relay(0)
    fan_arrived(2)
    spread(3)
    fan_arrived(3)
    spread(4)
    for index in range(1, PARTS + 1):
        relay(index)
    for d in (1, 2, 3):
        arrived(lab_in.at[d - 1], r_lab.at[d - 1])
        row = lab_in[d - 1, d - 1 : d, pl.ds(pl.multiple_of(x * 256, 256), 256)]
        lab_cols[d - 1] = jnp.broadcast_to(row, (8, 256))
    own_a.wait()
    own_b.wait()
    for o in (1, 2, 3):
        peer = lax.rem(x + o, 4)
        arrived(own.at[h, peer], r_own.at[peer])
        arrived(own.at[1 - h, peer], r_ob.at[peer])

    def wide(ref, *at):
        return jnp.concatenate(
            [ref[(*at, half, k)].reshape(-1, 128) for half in range(2) for k in range(4)], axis=1
        )

    def pair(slot):
        scores = lax.dot_general(
            wide(own), wide(q_ref, slot), (((1,), (1,)), ((), ())), preferred_element_type=jnp.float32
        )
        below = slot < OWN
        rows = lab_rows[jnp.where(below, OWN - 1 - slot, ROUNDS)]
        cols = lab_cols[jnp.where(below, ROUNDS, slot - OWN - 1)][:1]
        hit = jnp.concatenate([rows, rows], axis=1) == cols
        base = jnp.where(hit, -0.125, 0.125)
        slope[slot] = (0.125 * jnp.tanh(scores - 0.5) + base).astype(jnp.bfloat16)

    def slot_arrived(slot, delta, indices=range(PARTS + 1)):
        for index in indices:
            arrived(piece(slot, half_of(delta), index), r_z.at[slot, index])

    def step(i, _):
        slot = jnp.where(i == 0, 4 - 2 * c, 0)
        slot = jnp.where(i == 1, 1, slot)
        slot = jnp.where(i == 2, 5, slot)
        slot = jnp.where(i == 3, 2 - 2 * c, slot)
        slot = jnp.where(i == 4, 6 - 2 * c, slot)
        slot = jnp.where(i == 5, 6 * c, slot)

        @pl.when((i == 0) | (i > 2))
        def _():
            slot_arrived(slot, slot - OWN)

        pair(slot)
        return 0

    lax.fori_loop(0, 6, step, 0)

    def product(o):
        xd = lax.rem(x + o, 4)
        left = jnp.concatenate([slope[s] for s in SLOTS], axis=1)
        right = jnp.concatenate(
            [
                jnp.concatenate([q_ref[s, half, xd].reshape(256, 128) for half in range(2)], axis=1)
                for s in SLOTS
            ],
            axis=0,
        )
        value = jnp.dot(left, right, preferred_element_type=jnp.float32)
        for half in range(2):
            for t in range(4):
                tile = value[t * 128 : t * 128 + 128, half * 128 : half * 128 + 128]
                if o == 0 or (o != 2 and t in FULL):
                    part[o, t, half] = tile
                else:
                    small[o - 1, t, half] = tile.astype(jnp.bfloat16)

    def give(o, t):
        if o != 2 and t in FULL:
            send(part.at[o, t], got.at[o // 2, t // 2], r_got.at[o // 2, t // 2], beside(o))
        else:
            send(small.at[o - 1, t], got_small.at[o - 1, t], r_small.at[o - 1, t], beside(o))

    def finish(t):
        terms = []
        for o in (1, 2, 3):
            if o != 2 and t in FULL:
                arrived(got.at[o // 2, t // 2], r_got.at[o // 2, t // 2])
                terms.append((got, (o // 2, t // 2)))
            else:
                arrived(got_small.at[o - 1, t], r_small.at[o - 1, t])
                terms.append((got_small, (o - 1, t)))

        def total(half):
            value = part[0, t, half]
            for ref, at in terms:
                value = value + ref[(*at, half)].astype(jnp.float32)
            return value

        part[0, t, 1 - h] = total(1 - h)
        send(part.at[0, t, 1 - h], out_ref.at[h, t], r_out.at[t], across)
        out_ref[h, t] = total(h)

    product(2)
    for t in (0, 1):
        give(2, t)
    product(1)
    give(1, 0)
    product(3)
    give(3, 0)
    for o in (1, 3):
        give(o, 1)
    for t in (2, 3):
        for o in (2, 1, 3):
            give(o, t)
    product(0)
    for t in range(4):
        finish(t)
    for t in range(4):
        arrived(out_ref.at[1 - h, t], r_out.at[t])
    for copy in sent:
        copy.wait_send()
    for copy, inside in (leave(0), z != 7), (leave(1), z != 0), (leave(2), edge), (leave(3), edge):
        pl.when(inside)(copy.wait_send)


def shards(embeddings, labels):
    bf16, f32, dma = jnp.bfloat16, jnp.float32, pltpu.SemaphoreType.DMA
    block = (4, PARTS, ROWS, 128)
    out = pl.pallas_call(
        kernel,
        out_shape=jax.ShapeDtypeStruct((2, 4, 128, 128), f32),
        in_specs=[pl.BlockSpec(memory_space=pl.ANY)] * 2,
        out_specs=pl.BlockSpec(memory_space=pltpu.VMEM),
        scratch_shapes=[
            pltpu.VMEM(block, bf16),
            pltpu.VMEM(labels.shape, jnp.int32),
            pltpu.VMEM(block, bf16),
            pltpu.VMEM(block, bf16),
            pltpu.VMEM((7, 2) + block, bf16),
            pltpu.VMEM((2, 4, 2) + block[1:], bf16),
            pltpu.VMEM((7, 512, 256), bf16),
            pltpu.VMEM((ROUNDS + 1, 512, 128), jnp.int32),
            pltpu.VMEM((ROUNDS + 1, 8, 256), jnp.int32),
            pltpu.VMEM((ROUNDS,) + labels.shape, jnp.int32),
            pltpu.VMEM((4, 4, 2, 128, 128), f32),
            pltpu.VMEM((3, 4, 2, 128, 128), bf16),
            pltpu.VMEM((2, 2, 2, 128, 128), f32),
            pltpu.VMEM((3, 4, 2, 128, 128), bf16),
            dma((128,)), dma((3 + PARTS,)), dma((PARTS,)), dma((4,)), dma((4, PARTS)), dma((4,)),
            dma((4,)), dma((7, PARTS + 1)), dma((1,)), dma((3,)), dma((2, 2)), dma((3, 4)), dma((4,)),
        ],
        compiler_params=pltpu.CompilerParams(
            collective_id=0, has_side_effects=True, vmem_limit_bytes=40 * 2**20
        ),
    )(embeddings.reshape(block), labels)
    return out.reshape(1024, 128)


def solution(mesh):
    return jax.shard_map(
        shards,
        mesh=mesh,
        in_specs=(P("play", "col"), P(None, "play")),
        out_specs=P("play", "col"),
        check_vma=False,
    )
```

```python
import jax
import jax.numpy as jnp
from jax import lax
from jax.experimental import pallas as pl
from jax.experimental.pallas import tpu as pltpu
from jax.sharding import PartitionSpec as P

MESH = pl.DeviceIdType.MESH
OWN = 3
SLOTS = (0, 1, 2, 4, 5, 6)
ROUNDS = 3
PARTS = 4
ROWS = 256 // PARTS
FULL = (3,)


def kernel(
    e_hbm, lab_hbm, out_ref,
    e_ref, lab_ref, far, hop, q_ref, own, extra, slope, lab_rows, lab_cols, lab_in,
    part, small, got, got_small,
    send_sem, local_sem, r_far, r_qa, r_qb, r_own, r_ob, r_ex, r_z, r_hop, r_lab, r_got, r_small, r_out,
):
    play, col = lax.axis_index("play"), lax.axis_index("col")
    x, h = lax.rem(col, 4), col // 4
    c = lax.rem(play, 2)
    line = h * 64 + play

    def along(delta):
        to = lax.rem(line + delta + 128, 128)
        return {"play": lax.rem(to, 64), "col": (to // 64) * 4 + x}

    def beside(delta):
        return {"play": play, "col": h * 4 + lax.rem(x + delta, 4)}

    def half_of(delta):
        return lax.rem(line + delta + 128, 128) // 64

    across = {"play": play, "col": (1 - h) * 4 + x}
    twin = {"play": play + 1 - 2 * c, "col": col}

    barrier = pltpu.get_barrier_semaphore()
    greeted = [along(d) for d in (-3, -2, -1, 1, 2, 3)] + [beside(o) for o in (1, 2, 3)] + [across]
    for device in greeted:
        pl.semaphore_signal(barrier, inc=1, device_id=device, device_id_type=MESH)

    z = lax.rem(play // 2, 8)
    edge = (z == 0) | (z == 7)
    other_end = along(jnp.where(z == 0, 14, -14))
    onward = jnp.where(z == 0, 16, -16)

    @pl.when(edge)
    def _():
        for device in (other_end, along(16), along(-16)):
            pl.semaphore_signal(barrier, inc=1, device_id=device, device_id_type=MESH)

    sent = []

    def send(src, dst, recv, device):
        copy = pltpu.make_async_remote_copy(
            src_ref=src, dst_ref=dst, send_sem=send_sem.at[len(sent)], recv_sem=recv,
            device_id=device, device_id_type=MESH,
        )
        copy.start()
        sent.append(copy)

    def arrived(dst, recv):
        pltpu.make_async_copy(dst, dst, recv).wait()

    def place(src, dst, index):
        copy = pltpu.make_async_copy(src, dst, local_sem.at[index])
        copy.start()
        return copy

    fetch_lab = place(lab_hbm, lab_ref, 0)
    fetch_e = place(e_hbm, e_ref, 1)
    fetch_lab.wait()

    other = (1 - h) * 512 + 384
    for at, size, start in (0, 512, h * 512), (512, 128, other):
        lab = lab_ref[:, pl.ds(pl.multiple_of(start, 128), size)]
        lab = jnp.concatenate([lab, jnp.zeros((8 - ROUNDS, size), jnp.int32)], axis=0).T
        for r in range(ROUNDS):
            lab_rows[r, at : at + size] = jnp.broadcast_to(lab[:, r : r + 1], (size, 128))
        lab_rows[ROUNDS, at : at + size] = lax.broadcasted_iota(jnp.int32, (size, 128), 0) + start
    lab_cols[ROUNDS] = lax.broadcasted_iota(jnp.int32, (8, 256), 1) + x * 256
    fetch_e.wait()
    pl.semaphore_wait(barrier, jnp.where(edge, len(greeted) + 3, len(greeted)))

    for j in range(PARTS):
        send(e_ref.at[:, j], far.at[:, j], r_far.at[j], across)
    for o in (2, 1, 3):
        send(e_ref.at[lax.rem(x + o, 4)], q_ref.at[OWN, h, x], r_qa.at[x], beside(o))
    mine_a = place(e_ref.at[x], q_ref.at[OWN, h, x], 0)
    for d in (1, 2, 3):
        send(lab_ref, lab_in.at[d - 1], r_lab.at[d - 1], along(-d))
    for o in (2, 1, 3):
        send(e_ref.at[pl.ds(2 * h, 2)], own.at[h, x], r_own.at[x], beside(o))
    own_a = place(e_ref.at[pl.ds(2 * h, 2)], own.at[h, x], 1)
    late = (3 - 2 * h, pl.ds(PARTS // 2, PARTS // 2))
    for o in (2, 1, 3):
        send(e_ref.at[late], extra.at[h, x], r_ex.at[h, x], beside(o))
    extra_a = place(e_ref.at[late], extra.at[h, x], 3 + PARTS)

    def piece(slot, half, index):
        if index == 0:
            return q_ref.at[slot, half]
        return q_ref.at[slot, 1 - half, :, index - 1]

    def leave(way):
        slot = jnp.where(z == 0, 1, 5)
        src, dst, recv, device = (
            (piece(OWN, h, 0), piece(1, h, 0), r_z.at[1, 0], along(2)),
            (piece(OWN, h, 0), piece(5, h, 0), r_z.at[5, 0], along(-2)),
            (piece(OWN, h, 0), hop, r_hop.at[0], other_end),
            (hop, piece(slot, h, 0), r_z.at[slot, 0], along(onward)),
        )[way]
        return pltpu.make_async_remote_copy(
            src_ref=src, dst_ref=dst, send_sem=send_sem.at[124 + way], recv_sem=recv,
            device_id=device, device_id_type=MESH,
        )

    def spread(index):
        src = piece(OWN, h, index)
        if index == 0:
            for copy, inside in (leave(0), z != 7), (leave(1), z != 0), (leave(2), edge):
                pl.when(inside)(copy.start)
        else:
            send(src, piece(1, h, index), r_z.at[1, index], along(2))
            send(src, piece(5, h, index), r_z.at[5, index], along(-2))
        slot = 2 + 2 * c
        send(src, piece(slot, h, index), r_z.at[slot, index], twin)

    def relay(index):
        below, above = half_of(-2), half_of(2)
        arrived(piece(1, below, index), r_z.at[1, index])
        arrived(piece(5, above, index), r_z.at[5, index])
        half = jnp.where(c == 1, below, above)
        src, dst = 5 - 4 * c, 6 - 6 * c
        send(piece(src, half, index), piece(dst, half, index), r_z.at[dst, index], along(2 * c - 1))
        dst = 2 * c
        send(piece(1, below, index), piece(dst, below, index), r_z.at[dst, index], twin)
        dst = 4 + 2 * c
        send(piece(5, above, index), piece(dst, above, index), r_z.at[dst, index], twin)

    def fan(j):
        arrived(far.at[:, j], r_far.at[j])
        for o in (2, 1, 3):
            send(far.at[lax.rem(x + o, 4), j], q_ref.at[OWN, 1 - h, x, j], r_qb.at[x, j], beside(o))
        place(far.at[x, j], q_ref.at[OWN, 1 - h, x, j], 2 + j)

    def fan_arrived(j):
        for o in (1, 2, 3):
            peer = lax.rem(x + o, 4)
            arrived(q_ref.at[OWN, 1 - h, peer, j], r_qb.at[peer, j])
        pltpu.make_async_copy(far.at[x, j], q_ref.at[OWN, 1 - h, x, j], local_sem.at[2 + j]).wait()

    for o in (1, 2, 3):
        peer = lax.rem(x + o, 4)
        arrived(q_ref.at[OWN, h, peer], r_qa.at[peer])
    mine_a.wait()
    spread(0)
    fan(0)

    fan(1)
    fan_arrived(0)
    spread(1)
    @pl.when(edge)
    def _():
        leave(2).wait_recv()
        leave(3).start()

    fan(2)
    fan_arrived(1)
    spread(2)
    fan(3)
    for o in (2, 1, 3):
        send(far.at[pl.ds(2 * h, 2)], own.at[1 - h, x], r_ob.at[x], beside(o))
    own_b = place(far.at[pl.ds(2 * h, 2)], own.at[1 - h, x], 2 + PARTS)
    for o in (2, 1, 3):
        send(far.at[late], extra.at[1 - h, x], r_ex.at[1 - h, x], beside(o))
    extra_b = place(far.at[late], extra.at[1 - h, x], 4 + PARTS)
    relay(0)
    fan_arrived(2)
    spread(3)
    fan_arrived(3)
    spread(4)
    for index in range(1, PARTS + 1):
        relay(index)
    for d in (1, 2, 3):
        arrived(lab_in.at[d - 1], r_lab.at[d - 1])
        row = lab_in[d - 1, d - 1 : d, pl.ds(pl.multiple_of(x * 256, 256), 256)]
        lab_cols[d - 1] = jnp.broadcast_to(row, (8, 256))
    own_a.wait()
    own_b.wait()
    extra_a.wait()
    extra_b.wait()
    for o in (1, 2, 3):
        peer = lax.rem(x + o, 4)
        arrived(own.at[h, peer], r_own.at[peer])
        arrived(own.at[1 - h, peer], r_ob.at[peer])
        for half in range(2):
            arrived(extra.at[half, peer], r_ex.at[half, peer])

    def wide(ref, *at):
        return jnp.concatenate(
            [ref[(*at, half, k)].reshape(-1, 128) for half in range(2) for k in range(4)], axis=1
        )

    def pair(slot):
        scores = lax.dot_general(
            jnp.concatenate([wide(own), wide(extra)], axis=0), wide(q_ref, slot), (((1,), (1,)), ((), ())), preferred_element_type=jnp.float32
        )
        below = slot < OWN
        rows = lab_rows[jnp.where(below, OWN - 1 - slot, ROUNDS)]
        cols = lab_cols[jnp.where(below, ROUNDS, slot - OWN - 1)][:1]
        hit = jnp.concatenate([rows, rows], axis=1) == cols
        base = jnp.where(hit, -0.125, 0.125)
        slope[slot] = (0.125 * jnp.tanh(scores - 0.5) + base).astype(jnp.bfloat16)

    def slot_arrived(slot, delta, indices=range(PARTS + 1)):
        for index in indices:
            arrived(piece(slot, half_of(delta), index), r_z.at[slot, index])

    def step(i, _):
        slot = jnp.where(i == 0, 4 - 2 * c, 0)
        slot = jnp.where(i == 1, 1, slot)
        slot = jnp.where(i == 2, 5, slot)
        slot = jnp.where(i == 3, 2 - 2 * c, slot)
        slot = jnp.where(i == 4, 6 - 2 * c, slot)
        slot = jnp.where(i == 5, 6 * c, slot)

        @pl.when((i == 0) | (i > 2))
        def _():
            slot_arrived(slot, slot - OWN)

        pair(slot)
        return 0

    lax.fori_loop(0, 6, step, 0)

    def product(o):
        xd = lax.rem(x + o, 4)
        left = jnp.concatenate([slope[s] for s in SLOTS], axis=1)
        right = jnp.concatenate(
            [
                jnp.concatenate([q_ref[s, half, xd].reshape(256, 128) for half in (h, 1 - h)], axis=1)
                for s in SLOTS
            ],
            axis=0,
        )
        value = jnp.dot(left, right, preferred_element_type=jnp.float32)
        for t in range(4):
            for k in range(2):
                row, column = (t * 128, k * 128) if t < 3 else (384 + k * 128, 0)
                tile = value[row : row + 128, column : column + 128]
                if o == 0 or (o != 2 and t in FULL):
                    part[o, t, k] = tile
                else:
                    small[o - 1, t, k] = tile.astype(jnp.bfloat16)

    def give(o, t):
        if o != 2 and t in FULL:
            send(part.at[o, t], got.at[o // 2, FULL.index(t)], r_got.at[o // 2, FULL.index(t)], beside(o))
        else:
            send(small.at[o - 1, t], got_small.at[o - 1, t], r_small.at[o - 1, t], beside(o))

    def finish(t):
        terms = []
        for o in (1, 2, 3):
            if o != 2 and t in FULL:
                arrived(got.at[o // 2, FULL.index(t)], r_got.at[o // 2, FULL.index(t)])
                terms.append((got, (o // 2, FULL.index(t))))
            else:
                arrived(got_small.at[o - 1, t], r_small.at[o - 1, t])
                terms.append((got_small, (o - 1, t)))

        def total(half):
            value = part[0, t, half]
            for ref, at in terms:
                value = value + ref[(*at, half)].astype(jnp.float32)
            return value

        if t < 3:
            part[0, t, 1] = total(1)
            send(part.at[0, t, 1], out_ref.at[h, t], r_out.at[t], across)
        else:
            out_ref[1 - h, t] = total(1)
        out_ref[h, t] = total(0)

    product(2)
    for t in (0, 1):
        give(2, t)
    product(1)
    give(1, 0)
    product(3)
    give(3, 0)
    for o in (1, 3):
        give(o, 1)
    for t in (2, 3):
        for o in (2, 1, 3):
            give(o, t)
    product(0)
    for t in range(4):
        finish(t)
    for t in range(3):
        arrived(out_ref.at[1 - h, t], r_out.at[t])
    for copy in sent:
        copy.wait_send()
    for copy, inside in (leave(0), z != 7), (leave(1), z != 0), (leave(2), edge), (leave(3), edge):
        pl.when(inside)(copy.wait_send)


def shards(embeddings, labels):
    bf16, f32, dma = jnp.bfloat16, jnp.float32, pltpu.SemaphoreType.DMA
    block = (4, PARTS, ROWS, 128)
    out = pl.pallas_call(
        kernel,
        out_shape=jax.ShapeDtypeStruct((2, 4, 128, 128), f32),
        in_specs=[pl.BlockSpec(memory_space=pl.ANY)] * 2,
        out_specs=pl.BlockSpec(memory_space=pltpu.VMEM),
        scratch_shapes=[
            pltpu.VMEM(block, bf16),
            pltpu.VMEM(labels.shape, jnp.int32),
            pltpu.VMEM(block, bf16),
            pltpu.VMEM(block, bf16),
            pltpu.VMEM((7, 2) + block, bf16),
            pltpu.VMEM((2, 4, 2) + block[1:], bf16),
            pltpu.VMEM((2, 4, PARTS // 2) + block[2:], bf16),
            pltpu.VMEM((7, 640, 256), bf16),
            pltpu.VMEM((ROUNDS + 1, 640, 128), jnp.int32),
            pltpu.VMEM((ROUNDS + 1, 8, 256), jnp.int32),
            pltpu.VMEM((ROUNDS,) + labels.shape, jnp.int32),
            pltpu.VMEM((4, 4, 2, 128, 128), f32),
            pltpu.VMEM((3, 4, 2, 128, 128), bf16),
            pltpu.VMEM((2, len(FULL), 2, 128, 128), f32),
            pltpu.VMEM((3, 4, 2, 128, 128), bf16),
            dma((128,)), dma((5 + PARTS,)), dma((PARTS,)), dma((4,)), dma((4, PARTS)), dma((4,)),
            dma((4,)), dma((2, 4)), dma((7, PARTS + 1)), dma((1,)), dma((3,)), dma((2, len(FULL))), dma((3, 4)), dma((3,)),
        ],
        compiler_params=pltpu.CompilerParams(
            collective_id=0, has_side_effects=True, vmem_limit_bytes=40 * 2**20
        ),
    )(embeddings.reshape(block), labels)
    return out.reshape(1024, 128)


def solution(mesh):
    return jax.shard_map(
        shards,
        mesh=mesh,
        in_specs=(P("play", "col"), P(None, "play")),
        out_specs=P("play", "col"),
        check_vma=False,
    )
```

```python
import jax
import jax.numpy as jnp
from jax import lax
from jax.experimental import pallas as pl
from jax.experimental.pallas import tpu as pltpu
from jax.sharding import PartitionSpec as P

MESH = pl.DeviceIdType.MESH
OWN = 3
SLOTS = (0, 1, 2, 4, 5, 6)
ROUNDS = 3
PARTS = 4
ROWS = 256 // PARTS
PARCELS = ((1, 0, 1), (1, 1, 3), (0, 0, 3))


def kernel(
    e_hbm, lab_hbm, out_ref,
    e_ref, lab_ref, far, hop, q_ref, own, extra, slope, lab_rows, lab_cols, lab_in,
    part, small, got, got_small,
    send_sem, local_sem, r_far, r_qa, r_qb, r_own, r_ob, r_ex, r_z, r_hop, r_lab, r_small, r_out,
):
    play, col = lax.axis_index("play"), lax.axis_index("col")
    x, h = lax.rem(col, 4), col // 4
    c = lax.rem(play, 2)
    line = h * 64 + play

    def along(delta):
        to = lax.rem(line + delta + 128, 128)
        return {"play": lax.rem(to, 64), "col": (to // 64) * 4 + x}

    def beside(delta):
        return {"play": play, "col": h * 4 + lax.rem(x + delta, 4)}

    def half_of(delta):
        return lax.rem(line + delta + 128, 128) // 64

    across = {"play": play, "col": (1 - h) * 4 + x}
    twin = {"play": play + 1 - 2 * c, "col": col}

    barrier = pltpu.get_barrier_semaphore()
    greeted = [along(d) for d in (-3, -2, -1, 1, 2, 3)] + [beside(o) for o in (1, 2, 3)] + [across]
    for device in greeted:
        pl.semaphore_signal(barrier, inc=1, device_id=device, device_id_type=MESH)

    z = lax.rem(play // 2, 8)
    edge = (z == 0) | (z == 7)
    other_end = along(jnp.where(z == 0, 14, -14))
    onward = jnp.where(z == 0, 16, -16)

    @pl.when(edge)
    def _():
        for device in (other_end, along(16), along(-16)):
            pl.semaphore_signal(barrier, inc=1, device_id=device, device_id_type=MESH)

    sent = []

    def send(src, dst, recv, device):
        copy = pltpu.make_async_remote_copy(
            src_ref=src, dst_ref=dst, send_sem=send_sem.at[len(sent)], recv_sem=recv,
            device_id=device, device_id_type=MESH,
        )
        copy.start()
        sent.append(copy)

    def arrived(dst, recv):
        pltpu.make_async_copy(dst, dst, recv).wait()

    def place(src, dst, index):
        copy = pltpu.make_async_copy(src, dst, local_sem.at[index])
        copy.start()
        return copy

    fetch_lab = place(lab_hbm, lab_ref, 0)
    fetch_e = place(e_hbm, e_ref, 1)
    fetch_lab.wait()

    other = (1 - h) * 512 + 384
    for at, size, start in (0, 512, h * 512), (512, 128, other):
        lab = lab_ref[:, pl.ds(pl.multiple_of(start, 128), size)]
        lab = jnp.concatenate([lab, jnp.zeros((8 - ROUNDS, size), jnp.int32)], axis=0).T
        for r in range(ROUNDS):
            lab_rows[r, at : at + size] = jnp.broadcast_to(lab[:, r : r + 1], (size, 128))
        lab_rows[ROUNDS, at : at + size] = lax.broadcasted_iota(jnp.int32, (size, 128), 0) + start
    lab_cols[ROUNDS] = lax.broadcasted_iota(jnp.int32, (8, 256), 1) + x * 256
    fetch_e.wait()
    pl.semaphore_wait(barrier, jnp.where(edge, len(greeted) + 3, len(greeted)))

    for j in range(PARTS):
        send(e_ref.at[:, j], far.at[:, j], r_far.at[j], across)
    for o in (2, 1, 3):
        send(e_ref.at[lax.rem(x + o, 4)], q_ref.at[OWN, h, x], r_qa.at[x], beside(o))
    mine_a = place(e_ref.at[x], q_ref.at[OWN, h, x], 0)
    for d in (1, 2, 3):
        send(lab_ref, lab_in.at[d - 1], r_lab.at[d - 1], along(-d))
    for o in (2, 1, 3):
        send(e_ref.at[pl.ds(2 * h, 2)], own.at[h, x], r_own.at[x], beside(o))
    own_a = place(e_ref.at[pl.ds(2 * h, 2)], own.at[h, x], 1)
    late = (3 - 2 * h, pl.ds(PARTS // 2, PARTS // 2))
    for o in (2, 1, 3):
        send(e_ref.at[late], extra.at[h, x], r_ex.at[h, x], beside(o))
    extra_a = place(e_ref.at[late], extra.at[h, x], 3 + PARTS)

    def piece(slot, half, index):
        if index == 0:
            return q_ref.at[slot, half]
        return q_ref.at[slot, 1 - half, :, index - 1]

    def leave(way):
        slot = jnp.where(z == 0, 1, 5)
        src, dst, recv, device = (
            (piece(OWN, h, 0), piece(1, h, 0), r_z.at[1, 0], along(2)),
            (piece(OWN, h, 0), piece(5, h, 0), r_z.at[5, 0], along(-2)),
            (piece(OWN, h, 0), hop, r_hop.at[0], other_end),
            (hop, piece(slot, h, 0), r_z.at[slot, 0], along(onward)),
        )[way]
        return pltpu.make_async_remote_copy(
            src_ref=src, dst_ref=dst, send_sem=send_sem.at[124 + way], recv_sem=recv,
            device_id=device, device_id_type=MESH,
        )

    def spread(index):
        src = piece(OWN, h, index)
        if index == 0:
            for copy, inside in (leave(0), z != 7), (leave(1), z != 0), (leave(2), edge):
                pl.when(inside)(copy.start)
        else:
            send(src, piece(1, h, index), r_z.at[1, index], along(2))
            send(src, piece(5, h, index), r_z.at[5, index], along(-2))
        slot = 2 + 2 * c
        send(src, piece(slot, h, index), r_z.at[slot, index], twin)

    def relay(index):
        below, above = half_of(-2), half_of(2)
        arrived(piece(1, below, index), r_z.at[1, index])
        arrived(piece(5, above, index), r_z.at[5, index])
        half = jnp.where(c == 1, below, above)
        src, dst = 5 - 4 * c, 6 - 6 * c
        send(piece(src, half, index), piece(dst, half, index), r_z.at[dst, index], along(2 * c - 1))
        dst = 2 * c
        send(piece(1, below, index), piece(dst, below, index), r_z.at[dst, index], twin)
        dst = 4 + 2 * c
        send(piece(5, above, index), piece(dst, above, index), r_z.at[dst, index], twin)

    def fan(j):
        arrived(far.at[:, j], r_far.at[j])
        for o in (2, 1, 3):
            send(far.at[lax.rem(x + o, 4), j], q_ref.at[OWN, 1 - h, x, j], r_qb.at[x, j], beside(o))
        place(far.at[x, j], q_ref.at[OWN, 1 - h, x, j], 2 + j)

    def fan_arrived(j):
        for o in (1, 2, 3):
            peer = lax.rem(x + o, 4)
            arrived(q_ref.at[OWN, 1 - h, peer, j], r_qb.at[peer, j])
        pltpu.make_async_copy(far.at[x, j], q_ref.at[OWN, 1 - h, x, j], local_sem.at[2 + j]).wait()

    for o in (1, 2, 3):
        peer = lax.rem(x + o, 4)
        arrived(q_ref.at[OWN, h, peer], r_qa.at[peer])
    mine_a.wait()
    spread(0)
    fan(0)
    fan(1)
    fan_arrived(0)
    spread(1)
    fan(2)
    @pl.when(edge)
    def _():
        leave(2).wait_recv()
        leave(3).start()

    fan(3)
    fan_arrived(1)
    spread(2)
    for o in (2, 1, 3):
        send(far.at[pl.ds(2 * h, 2)], own.at[1 - h, x], r_ob.at[x], beside(o))
    own_b = place(far.at[pl.ds(2 * h, 2)], own.at[1 - h, x], 2 + PARTS)
    for o in (2, 1, 3):
        send(far.at[late], extra.at[1 - h, x], r_ex.at[1 - h, x], beside(o))
    extra_b = place(far.at[late], extra.at[1 - h, x], 4 + PARTS)
    fan_arrived(2)
    spread(3)
    fan_arrived(3)
    spread(4)
    relay(1)
    relay(2)
    relay(0)
    relay(3)
    relay(4)
    for d in (1, 2, 3):
        arrived(lab_in.at[d - 1], r_lab.at[d - 1])
        row = lab_in[d - 1, d - 1 : d, pl.ds(pl.multiple_of(x * 256, 256), 256)]
        lab_cols[d - 1] = jnp.broadcast_to(row, (8, 256))
    own_a.wait()
    own_b.wait()
    extra_a.wait()
    extra_b.wait()
    for o in (1, 2, 3):
        peer = lax.rem(x + o, 4)
        arrived(own.at[h, peer], r_own.at[peer])
        arrived(own.at[1 - h, peer], r_ob.at[peer])
        for half in range(2):
            arrived(extra.at[half, peer], r_ex.at[half, peer])

    def wide(ref, *at):
        return jnp.concatenate(
            [ref[(*at, half, k)].reshape(-1, 128) for half in range(2) for k in range(4)], axis=1
        )

    def pair(slot):
        scores = lax.dot_general(
            jnp.concatenate([wide(own), wide(extra)], axis=0), wide(q_ref, slot), (((1,), (1,)), ((), ())), preferred_element_type=jnp.float32
        )
        below = slot < OWN
        rows = lab_rows[jnp.where(below, OWN - 1 - slot, ROUNDS)]
        cols = lab_cols[jnp.where(below, ROUNDS, slot - OWN - 1)][:1]
        hit = jnp.concatenate([rows, rows], axis=1) == cols
        base = jnp.where(hit, -0.125, 0.125)
        slope[slot] = (0.125 * jnp.tanh(scores - 0.5) + base).astype(jnp.bfloat16)

    def slot_arrived(slot, delta, indices=range(PARTS + 1)):
        for index in indices:
            arrived(piece(slot, half_of(delta), index), r_z.at[slot, index])

    def step(i, _):
        slot = jnp.where(i == 0, 4 - 2 * c, 0)
        slot = jnp.where(i == 1, 1, slot)
        slot = jnp.where(i == 2, 5, slot)
        slot = jnp.where(i == 3, 2 - 2 * c, slot)
        slot = jnp.where(i == 4, 6 - 2 * c, slot)
        slot = jnp.where(i == 5, 6 * c, slot)

        @pl.when((i == 0) | (i > 2))
        def _():
            slot_arrived(slot, slot - OWN)

        pair(slot)
        return 0

    lax.fori_loop(0, 6, step, 0)

    def product(o):
        xd = lax.rem(x + o, 4)
        left = jnp.concatenate([slope[s] for s in SLOTS], axis=1)
        right = jnp.concatenate(
            [
                jnp.concatenate([q_ref[s, half, xd].reshape(256, 128) for half in (h, 1 - h)], axis=1)
                for s in SLOTS
            ],
            axis=0,
        )
        value = jnp.dot(left, right, preferred_element_type=jnp.float32)
        for t in range(4):
            for k in range(2):
                row, column = (t * 128, k * 128) if t < 3 else (384 + k * 128, 0)
                tile = value[row : row + 128, column : column + 128]
                if o == 0 or (o != 2 and t == 3):
                    part[o, t, k] = tile
                else:
                    small[o - 1, k, t] = tile.astype(jnp.bfloat16)

    def parcel(o, m):
        if m < 3:
            k, first, end = PARCELS[m]
            at = (o - 1, k, pl.ds(first, end - first))
            return small.at[at], got_small.at[at], r_small.at[o - 1, m]
        if o == 2:
            return small.at[1, :, 3], got_small.at[1, :, 3], r_small.at[1, 3]
        return part.at[o, 3], got.at[o // 2], r_small.at[o - 1, 3]

    def give(o, m):
        send(*parcel(o, m), beside(o))

    def take(m):
        for o in (1, 2, 3):
            _, dst, recv = parcel(o, m)
            arrived(dst, recv)

    def total(t, k):
        value = part[0, t, k] + got_small[1, k, t].astype(jnp.float32)
        if t == 3:
            return value + got[0, k] + got[1, k]
        return value + got_small[0, k, t].astype(jnp.float32) + got_small[2, k, t].astype(jnp.float32)

    def finish(m):
        take(m)
        if m == 3:
            out_ref[h, 3] = total(3, 0)
            out_ref[1 - h, 3] = total(3, 1)
            return
        k, first, end = PARCELS[m]
        for t in range(first, end):
            if k == 1:
                part[0, t, 1] = total(t, 1)
            else:
                out_ref[h, t] = total(t, 0)
        if k == 1:
            rows = pl.ds(first, end - first)
            send(part.at[0, rows, 1], out_ref.at[h, rows], r_out.at[m], across)

    product(2)
    give(2, 0)
    product(1)
    give(1, 0)
    give(2, 1)
    product(3)
    give(3, 0)
    give(1, 1)
    give(3, 1)
    for m in (2, 3):
        for o in (2, 1, 3):
            give(o, m)
    product(0)
    for m in range(4):
        finish(m)
    for k, first, end in PARCELS[:2]:
        arrived(out_ref.at[1 - h, pl.ds(first, end - first)], r_out.at[first])
    for copy in sent:
        copy.wait_send()
    for copy, inside in (leave(0), z != 7), (leave(1), z != 0), (leave(2), edge), (leave(3), edge):
        pl.when(inside)(copy.wait_send)


def shards(embeddings, labels):
    bf16, f32, dma = jnp.bfloat16, jnp.float32, pltpu.SemaphoreType.DMA
    block = (4, PARTS, ROWS, 128)
    out = pl.pallas_call(
        kernel,
        out_shape=jax.ShapeDtypeStruct((2, 4, 128, 128), f32),
        in_specs=[pl.BlockSpec(memory_space=pl.ANY)] * 2,
        out_specs=pl.BlockSpec(memory_space=pltpu.VMEM),
        scratch_shapes=[
            pltpu.VMEM(block, bf16),
            pltpu.VMEM(labels.shape, jnp.int32),
            pltpu.VMEM(block, bf16),
            pltpu.VMEM(block, bf16),
            pltpu.VMEM((7, 2) + block, bf16),
            pltpu.VMEM((2, 4, 2) + block[1:], bf16),
            pltpu.VMEM((2, 4, PARTS // 2) + block[2:], bf16),
            pltpu.VMEM((7, 640, 256), bf16),
            pltpu.VMEM((ROUNDS + 1, 640, 128), jnp.int32),
            pltpu.VMEM((ROUNDS + 1, 8, 256), jnp.int32),
            pltpu.VMEM((ROUNDS,) + labels.shape, jnp.int32),
            pltpu.VMEM((4, 4, 2, 128, 128), f32),
            pltpu.VMEM((3, 2, 4, 128, 128), bf16),
            pltpu.VMEM((2, 2, 128, 128), f32),
            pltpu.VMEM((3, 2, 4, 128, 128), bf16),
            dma((128,)), dma((5 + PARTS,)), dma((PARTS,)), dma((4,)), dma((4, PARTS)), dma((4,)),
            dma((4,)), dma((2, 4)), dma((7, PARTS + 1)), dma((1,)), dma((3,)), dma((3, 4)), dma((2,)),
        ],
        compiler_params=pltpu.CompilerParams(
            collective_id=0, has_side_effects=True, vmem_limit_bytes=40 * 2**20
        ),
    )(embeddings.reshape(block), labels)
    return out.reshape(1024, 128)


def solution(mesh):
    return jax.shard_map(
        shards,
        mesh=mesh,
        in_specs=(P("play", "col"), P(None, "play")),
        out_specs=P("play", "col"),
        check_vma=False,
    )
```

```python
import jax
import jax.numpy as jnp
from jax import lax
from jax.experimental import pallas as pl
from jax.experimental.pallas import tpu as pltpu
from jax.sharding import PartitionSpec as P

MESH = pl.DeviceIdType.MESH
OWN = 3
SLOTS = (0, 1, 2, 4, 5, 6)
ROUNDS = 3
STRIPES, ROWS = 4, 64
CUTS = ((0, 2), (2, 1), (3, 1))
PARTS = len(CUTS)
PARCELS = ((1, 0, 1), (1, 1, 2), (1, 2, 3), (0, 0, 3))
LAST = len(PARCELS)


def kernel(
    e_hbm, lab_hbm, out_ref,
    e_ref, lab_ref, far, hop, q_ref, own, extra, slope, lab_rows, lab_cols, lab_in,
    part, small, got, got_small,
    send_sem, local_sem, r_far, r_qa, r_qb, r_own, r_ob, r_ex, r_z, r_hop, r_lab, r_small, r_out,
):
    play, col = lax.axis_index("play"), lax.axis_index("col")
    x, h = lax.rem(col, 4), col // 4
    c = lax.rem(play, 2)
    line = h * 64 + play

    def along(delta):
        to = lax.rem(line + delta + 128, 128)
        return {"play": lax.rem(to, 64), "col": (to // 64) * 4 + x}

    def beside(delta):
        return {"play": play, "col": h * 4 + lax.rem(x + delta, 4)}

    def half_of(delta):
        return lax.rem(line + delta + 128, 128) // 64

    across = {"play": play, "col": (1 - h) * 4 + x}
    twin = {"play": play + 1 - 2 * c, "col": col}

    barrier = pltpu.get_barrier_semaphore()
    greeted = [along(d) for d in (-3, -2, -1, 1, 2, 3)] + [beside(o) for o in (1, 2, 3)] + [across]
    for device in greeted:
        pl.semaphore_signal(barrier, inc=1, device_id=device, device_id_type=MESH)

    z = lax.rem(play // 2, 8)
    edge = (z == 0) | (z == 7)
    other_end = along(jnp.where(z == 0, 14, -14))
    onward = jnp.where(z == 0, 16, -16)

    @pl.when(edge)
    def _():
        for device in (other_end, along(16), along(-16)):
            pl.semaphore_signal(barrier, inc=1, device_id=device, device_id_type=MESH)

    sent = []

    def send(src, dst, recv, device):
        copy = pltpu.make_async_remote_copy(
            src_ref=src, dst_ref=dst, send_sem=send_sem.at[len(sent)], recv_sem=recv,
            device_id=device, device_id_type=MESH,
        )
        copy.start()
        sent.append(copy)

    def arrived(dst, recv):
        pltpu.make_async_copy(dst, dst, recv).wait()

    def place(src, dst, index):
        copy = pltpu.make_async_copy(src, dst, local_sem.at[index])
        copy.start()
        return copy

    fetch_lab = place(lab_hbm, lab_ref, 0)
    fetch_e = place(e_hbm, e_ref, 1)
    fetch_lab.wait()

    other = (1 - h) * 512 + 384
    for at, size, start in (0, 512, h * 512), (512, 128, other):
        lab = lab_ref[:, pl.ds(pl.multiple_of(start, 128), size)]
        lab = jnp.concatenate([lab, jnp.zeros((8 - ROUNDS, size), jnp.int32)], axis=0).T
        for r in range(ROUNDS):
            lab_rows[r, at : at + size] = jnp.broadcast_to(lab[:, r : r + 1], (size, 128))
        lab_rows[ROUNDS, at : at + size] = lax.broadcasted_iota(jnp.int32, (size, 128), 0) + start
    lab_cols[ROUNDS] = lax.broadcasted_iota(jnp.int32, (8, 256), 1) + x * 256
    fetch_e.wait()
    pl.semaphore_wait(barrier, jnp.where(edge, len(greeted) + 3, len(greeted)))

    for j in range(PARTS):
        send(e_ref.at[:, pl.ds(*CUTS[j])], far.at[:, pl.ds(*CUTS[j])], r_far.at[j], across)
    for o in (2, 1, 3):
        send(e_ref.at[lax.rem(x + o, 4)], q_ref.at[OWN, h, x], r_qa.at[x], beside(o))
    mine_a = place(e_ref.at[x], q_ref.at[OWN, h, x], 0)
    for d in (1, 2, 3):
        send(lab_ref, lab_in.at[d - 1], r_lab.at[d - 1], along(-d))
    for o in (2, 1, 3):
        send(e_ref.at[pl.ds(2 * h, 2)], own.at[h, x], r_own.at[x], beside(o))
    own_a = place(e_ref.at[pl.ds(2 * h, 2)], own.at[h, x], 1)
    late = (3 - 2 * h, pl.ds(STRIPES // 2, STRIPES // 2))
    for o in (2, 1, 3):
        send(e_ref.at[late], extra.at[h, x], r_ex.at[h, x], beside(o))
    extra_a = place(e_ref.at[late], extra.at[h, x], 3 + PARTS)

    def piece(slot, half, index):
        if index == 0:
            return q_ref.at[slot, half]
        return q_ref.at[slot, 1 - half, :, pl.ds(*CUTS[index - 1])]

    def leave(way):
        slot = jnp.where(z == 0, 1, 5)
        src, dst, recv, device = (
            (piece(OWN, h, 0), piece(1, h, 0), r_z.at[1, 0], along(2)),
            (piece(OWN, h, 0), piece(5, h, 0), r_z.at[5, 0], along(-2)),
            (piece(OWN, h, 0), hop, r_hop.at[0], other_end),
            (hop, piece(slot, h, 0), r_z.at[slot, 0], along(onward)),
        )[way]
        return pltpu.make_async_remote_copy(
            src_ref=src, dst_ref=dst, send_sem=send_sem.at[124 + way], recv_sem=recv,
            device_id=device, device_id_type=MESH,
        )

    def spread(index):
        src = piece(OWN, h, index)
        if index == 0:
            for copy, inside in (leave(0), z != 7), (leave(1), z != 0), (leave(2), edge):
                pl.when(inside)(copy.start)
        else:
            send(src, piece(1, h, index), r_z.at[1, index], along(2))
            send(src, piece(5, h, index), r_z.at[5, index], along(-2))
        slot = 2 + 2 * c
        send(src, piece(slot, h, index), r_z.at[slot, index], twin)

    def relay(index):
        below, above = half_of(-2), half_of(2)
        half, rest = jnp.where(c == 1, below, above), jnp.where(c == 1, above, below)
        src, dst = 5 - 4 * c, 6 - 6 * c
        arrived(piece(src, half, index), r_z.at[src, index])
        send(piece(src, half, index), piece(dst, half, index), r_z.at[dst, index], along(2 * c - 1))
        dst = 4 - 2 * c
        send(piece(src, half, index), piece(dst, half, index), r_z.at[dst, index], twin)
        src, dst = 1 + 4 * c, 6 * c
        arrived(piece(src, rest, index), r_z.at[src, index])
        send(piece(src, rest, index), piece(dst, rest, index), r_z.at[dst, index], twin)

    def fan(j):
        part_of = pl.ds(*CUTS[j])
        arrived(far.at[:, part_of], r_far.at[j])
        for o in (2, 1, 3):
            send(far.at[lax.rem(x + o, 4), part_of], q_ref.at[OWN, 1 - h, x, part_of], r_qb.at[x, j], beside(o))
        place(far.at[x, part_of], q_ref.at[OWN, 1 - h, x, part_of], 2 + j)

    def fan_arrived(j):
        for o in (1, 2, 3):
            peer = lax.rem(x + o, 4)
            arrived(q_ref.at[OWN, 1 - h, peer, pl.ds(*CUTS[j])], r_qb.at[peer, j])
        arrived(q_ref.at[OWN, 1 - h, x, pl.ds(*CUTS[j])], local_sem.at[2 + j])

    for o in (1, 2, 3):
        peer = lax.rem(x + o, 4)
        arrived(q_ref.at[OWN, h, peer], r_qa.at[peer])
    mine_a.wait()
    spread(0)
    fan(0)
    fan(1)
    @pl.when(edge)
    def _():
        leave(2).wait_recv()
        leave(3).start()

    fan_arrived(0)
    spread(1)
    fan(2)
    for o in (2, 1, 3):
        send(far.at[pl.ds(2 * h, 2)], own.at[1 - h, x], r_ob.at[x], beside(o))
    own_b = place(far.at[pl.ds(2 * h, 2)], own.at[1 - h, x], 2 + PARTS)
    for o in (2, 1, 3):
        send(far.at[late], extra.at[1 - h, x], r_ex.at[1 - h, x], beside(o))
    extra_b = place(far.at[late], extra.at[1 - h, x], 4 + PARTS)
    fan_arrived(1)
    spread(2)
    fan_arrived(2)
    spread(3)
    relay(1)
    relay(0)
    relay(2)
    relay(3)
    for d in (1, 2, 3):
        arrived(lab_in.at[d - 1], r_lab.at[d - 1])
        row = lab_in[d - 1, d - 1 : d, pl.ds(pl.multiple_of(x * 256, 256), 256)]
        lab_cols[d - 1] = jnp.broadcast_to(row, (8, 256))
    own_a.wait()
    own_b.wait()
    extra_a.wait()
    extra_b.wait()
    for o in (1, 2, 3):
        peer = lax.rem(x + o, 4)
        arrived(own.at[h, peer], r_own.at[peer])
        arrived(own.at[1 - h, peer], r_ob.at[peer])
        for half in range(2):
            arrived(extra.at[half, peer], r_ex.at[half, peer])

    def wide(ref, *at):
        return jnp.concatenate(
            [ref[(*at, half, k)].reshape(-1, 128) for half in range(2) for k in range(4)], axis=1
        )

    def pair(slot):
        scores = lax.dot_general(
            jnp.concatenate([wide(own), wide(extra)], axis=0), wide(q_ref, slot), (((1,), (1,)), ((), ())), preferred_element_type=jnp.float32
        )
        below = slot < OWN
        rows = lab_rows[jnp.where(below, OWN - 1 - slot, ROUNDS)]
        cols = lab_cols[jnp.where(below, ROUNDS, slot - OWN - 1)][:1]
        hit = jnp.concatenate([rows, rows], axis=1) == cols
        base = jnp.where(hit, -0.125, 0.125)
        slope[slot] = (0.125 * jnp.tanh(scores - 0.5) + base).astype(jnp.bfloat16)

    def slot_arrived(slot, delta, indices=range(PARTS + 1)):
        for index in indices:
            arrived(piece(slot, half_of(delta), index), r_z.at[slot, index])

    def step(i, _):
        slot = jnp.where(i == 0, 4 - 2 * c, 0)
        slot = jnp.where(i == 1, 1, slot)
        slot = jnp.where(i == 2, 5, slot)
        slot = jnp.where(i == 3, 2 - 2 * c, slot)
        slot = jnp.where(i == 4, 6 - 2 * c, slot)
        slot = jnp.where(i == 5, 6 * c, slot)

        @pl.when((i == 0) | (i > 2))
        def _():
            slot_arrived(slot, slot - OWN)

        pair(slot)
        return 0

    lax.fori_loop(0, 6, step, 0)

    def product(o):
        xd = lax.rem(x + o, 4)
        left = jnp.concatenate([slope[s] for s in SLOTS], axis=1)
        right = jnp.concatenate(
            [
                jnp.concatenate([q_ref[s, half, xd].reshape(256, 128) for half in (h, 1 - h)], axis=1)
                for s in SLOTS
            ],
            axis=0,
        )
        value = jnp.dot(left, right, preferred_element_type=jnp.float32)
        for t in range(4):
            for k in range(2):
                row, column = (t * 128, k * 128) if t < 3 else (384 + k * 128, 0)
                tile = value[row : row + 128, column : column + 128]
                if o == 0 or (o != 2 and t == 3):
                    part[o, t, k] = tile
                else:
                    small[o - 1, k, t] = tile.astype(jnp.bfloat16)

    def parcel(o, m):
        if m < LAST:
            k, first, end = PARCELS[m]
            at = (o - 1, k, pl.ds(first, end - first))
            return small.at[at], got_small.at[at], r_small.at[o - 1, m]
        if o == 2:
            return small.at[1, :, 3], got_small.at[1, :, 3], r_small.at[1, LAST]
        return part.at[o, 3], got.at[o // 2], r_small.at[o - 1, LAST]

    def give(o, m):
        send(*parcel(o, m), beside(o))

    def take(m):
        for o in (1, 2, 3):
            _, dst, recv = parcel(o, m)
            arrived(dst, recv)

    def total(t, k):
        value = part[0, t, k] + got_small[1, k, t].astype(jnp.float32)
        if t == 3:
            return value + got[0, k] + got[1, k]
        return value + got_small[0, k, t].astype(jnp.float32) + got_small[2, k, t].astype(jnp.float32)

    def finish(m):
        take(m)
        if m == LAST:
            out_ref[h, 3] = total(3, 0)
            out_ref[1 - h, 3] = total(3, 1)
            return
        k, first, end = PARCELS[m]
        for t in range(first, end):
            if k == 1:
                part[0, t, 1] = total(t, 1)
            else:
                out_ref[h, t] = total(t, 0)
        if k == 1:
            rows = pl.ds(first, end - first)
            send(part.at[0, rows, 1], out_ref.at[h, rows], r_out.at[m], across)

    product(2)
    give(2, 0)
    product(1)
    give(1, 0)
    give(2, 1)
    product(3)
    give(3, 0)
    give(1, 1)
    give(3, 1)
    for m in range(2, LAST + 1):
        for o in (2, 1, 3):
            give(o, m)
    product(0)
    for m in range(LAST + 1):
        finish(m)
    for m in range(LAST):
        k, first, end = PARCELS[m]
        if k == 1:
            arrived(out_ref.at[1 - h, pl.ds(first, end - first)], r_out.at[m])
    for copy in sent:
        copy.wait_send()
    for copy, inside in (leave(0), z != 7), (leave(1), z != 0), (leave(2), edge), (leave(3), edge):
        pl.when(inside)(copy.wait_send)


def shards(embeddings, labels):
    bf16, f32, dma = jnp.bfloat16, jnp.float32, pltpu.SemaphoreType.DMA
    block = (4, STRIPES, ROWS, 128)
    out = pl.pallas_call(
        kernel,
        out_shape=jax.ShapeDtypeStruct((2, 4, 128, 128), f32),
        in_specs=[pl.BlockSpec(memory_space=pl.ANY)] * 2,
        out_specs=pl.BlockSpec(memory_space=pltpu.VMEM),
        scratch_shapes=[
            pltpu.VMEM(block, bf16),
            pltpu.VMEM(labels.shape, jnp.int32),
            pltpu.VMEM(block, bf16),
            pltpu.VMEM(block, bf16),
            pltpu.VMEM((7, 2) + block, bf16),
            pltpu.VMEM((2, 4, 2) + block[1:], bf16),
            pltpu.VMEM((2, 4, STRIPES // 2) + block[2:], bf16),
            pltpu.VMEM((7, 640, 256), bf16),
            pltpu.VMEM((ROUNDS + 1, 640, 128), jnp.int32),
            pltpu.VMEM((ROUNDS + 1, 8, 256), jnp.int32),
            pltpu.VMEM((ROUNDS,) + labels.shape, jnp.int32),
            pltpu.VMEM((4, 4, 2, 128, 128), f32),
            pltpu.VMEM((3, 2, 4, 128, 128), bf16),
            pltpu.VMEM((2, 2, 128, 128), f32),
            pltpu.VMEM((3, 2, 4, 128, 128), bf16),
            dma((128,)), dma((5 + PARTS,)), dma((PARTS,)), dma((4,)), dma((4, PARTS)), dma((4,)),
            dma((4,)), dma((2, 4)), dma((7, PARTS + 1)), dma((1,)), dma((3,)), dma((3, 6)), dma((4,)),
        ],
        compiler_params=pltpu.CompilerParams(
            collective_id=0, has_side_effects=True, vmem_limit_bytes=40 * 2**20
        ),
    )(embeddings.reshape(block), labels)
    return out.reshape(1024, 128)


def solution(mesh):
    return jax.shard_map(
        shards,
        mesh=mesh,
        in_specs=(P("play", "col"), P(None, "play")),
        out_specs=P("play", "col"),
        check_vma=False,
    )
```

```python
import jax
import jax.numpy as jnp
from jax import lax
from jax.experimental import pallas as pl
from jax.experimental.pallas import tpu as pltpu
from jax.sharding import PartitionSpec as P

MESH = pl.DeviceIdType.MESH
OWN = 3
SLOTS = (0, 1, 2, 4, 5, 6)
ROUNDS = 3
STRIPES, ROWS = 4, 64
CUTS = ((0, 2), (2, 1), (3, 1))
PARTS = len(CUTS)
PARCELS = ((1, 0, 1), (1, 1, 2), (1, 2, 3), (0, 0, 3))
LAST = len(PARCELS)


def kernel(
    e_hbm, lab_hbm, out_ref,
    e_ref, lab_ref, far, hop, q_ref, own, extra, slope, lab_rows, lab_cols, lab_in,
    part, small, got, got_small,
    send_sem, local_sem, r_far, r_qa, r_qb, r_own, r_ob, r_ex, r_z, r_hop, r_lab, r_small, r_out,
):
    play, col = lax.axis_index("play"), lax.axis_index("col")
    x, h = lax.rem(col, 4), col // 4
    c = lax.rem(play, 2)
    line = h * 64 + play

    def along(delta):
        to = lax.rem(line + delta + 128, 128)
        return {"play": lax.rem(to, 64), "col": (to // 64) * 4 + x}

    def beside(delta):
        return {"play": play, "col": h * 4 + lax.rem(x + delta, 4)}

    def half_of(delta):
        return lax.rem(line + delta + 128, 128) // 64

    across = {"play": play, "col": (1 - h) * 4 + x}
    twin = {"play": play + 1 - 2 * c, "col": col}

    barrier = pltpu.get_barrier_semaphore()
    greeted = [along(d) for d in (-3, -2, -1, 1, 2, 3)] + [beside(o) for o in (1, 2, 3)] + [across]
    for device in greeted:
        pl.semaphore_signal(barrier, inc=1, device_id=device, device_id_type=MESH)

    z = lax.rem(play // 2, 8)
    edge = (z == 0) | (z == 7)
    other_end = along(jnp.where(z == 0, 14, -14))
    onward = jnp.where(z == 0, 16, -16)

    @pl.when(edge)
    def _():
        for device in (other_end, along(16), along(-16)):
            pl.semaphore_signal(barrier, inc=1, device_id=device, device_id_type=MESH)

    sent = []

    def send(src, dst, recv, device):
        copy = pltpu.make_async_remote_copy(
            src_ref=src, dst_ref=dst, send_sem=send_sem.at[len(sent)], recv_sem=recv,
            device_id=device, device_id_type=MESH,
        )
        copy.start()
        sent.append(copy)

    def arrived(dst, recv):
        pltpu.make_async_copy(dst, dst, recv).wait()

    def place(src, dst, index):
        copy = pltpu.make_async_copy(src, dst, local_sem.at[index])
        copy.start()
        return copy

    fetch_lab = place(lab_hbm, lab_ref, 0)
    fetch_e = place(e_hbm, e_ref, 1)
    fetch_lab.wait()

    other = (1 - h) * 512 + 384
    for at, size, start in (0, 512, h * 512), (512, 128, other):
        lab = lab_ref[:, pl.ds(pl.multiple_of(start, 128), size)]
        lab = jnp.concatenate([lab, jnp.zeros((8 - ROUNDS, size), jnp.int32)], axis=0).T
        for r in range(ROUNDS):
            lab_rows[r, at : at + size] = jnp.broadcast_to(lab[:, r : r + 1], (size, 128))
        lab_rows[ROUNDS, at : at + size] = lax.broadcasted_iota(jnp.int32, (size, 128), 0) + start
    lab_cols[ROUNDS] = lax.broadcasted_iota(jnp.int32, (8, 256), 1) + x * 256
    fetch_e.wait()
    pl.semaphore_wait(barrier, jnp.where(edge, len(greeted) + 3, len(greeted)))

    for j in range(PARTS):
        send(e_ref.at[:, pl.ds(*CUTS[j])], far.at[:, pl.ds(*CUTS[j])], r_far.at[j], across)
    for o in (2, 1, 3):
        send(e_ref.at[lax.rem(x + o, 4)], q_ref.at[OWN, h, x], r_qa.at[x], beside(o))
    mine_a = place(e_ref.at[x], q_ref.at[OWN, h, x], 0)
    for d in (1, 2, 3):
        send(lab_ref, lab_in.at[d - 1], r_lab.at[d - 1], along(-d))
    for o in (2, 1, 3):
        send(e_ref.at[pl.ds(2 * h, 2)], own.at[h, x], r_own.at[x], beside(o))
    own_a = place(e_ref.at[pl.ds(2 * h, 2)], own.at[h, x], 1)
    late = (3 - 2 * h, pl.ds(STRIPES // 2, STRIPES // 2))
    for o in (2, 1, 3):
        send(e_ref.at[late], extra.at[h, x], r_ex.at[h, x], beside(o))
    extra_a = place(e_ref.at[late], extra.at[h, x], 3 + PARTS)

    def piece(slot, half, index):
        if index == 0:
            return q_ref.at[slot, half]
        return q_ref.at[slot, 1 - half, :, pl.ds(*CUTS[index - 1])]

    def leave(way):
        slot = jnp.where(z == 0, 1, 5)
        src, dst, recv, device = (
            (piece(OWN, h, 0), piece(1, h, 0), r_z.at[1, 0], along(2)),
            (piece(OWN, h, 0), piece(5, h, 0), r_z.at[5, 0], along(-2)),
            (piece(OWN, h, 0), hop, r_hop.at[0], other_end),
            (hop, piece(slot, h, 0), r_z.at[slot, 0], along(onward)),
        )[way]
        return pltpu.make_async_remote_copy(
            src_ref=src, dst_ref=dst, send_sem=send_sem.at[124 + way], recv_sem=recv,
            device_id=device, device_id_type=MESH,
        )

    def spread(index):
        src = piece(OWN, h, index)
        if index == 0:
            for copy, inside in (leave(0), z != 7), (leave(1), z != 0), (leave(2), edge):
                pl.when(inside)(copy.start)
        else:
            send(src, piece(1, h, index), r_z.at[1, index], along(2))
            send(src, piece(5, h, index), r_z.at[5, index], along(-2))
        slot = 2 + 2 * c
        send(src, piece(slot, h, index), r_z.at[slot, index], twin)

    def relay(index):
        below, above = half_of(-2), half_of(2)
        half, rest = jnp.where(c == 1, below, above), jnp.where(c == 1, above, below)
        src, dst = 5 - 4 * c, 6 - 6 * c
        arrived(piece(src, half, index), r_z.at[src, index])
        send(piece(src, half, index), piece(dst, half, index), r_z.at[dst, index], along(2 * c - 1))
        dst = 4 - 2 * c
        send(piece(src, half, index), piece(dst, half, index), r_z.at[dst, index], twin)
        src, dst = 1 + 4 * c, 6 * c
        arrived(piece(src, rest, index), r_z.at[src, index])
        send(piece(src, rest, index), piece(dst, rest, index), r_z.at[dst, index], twin)

    def fan(j):
        part_of = pl.ds(*CUTS[j])
        arrived(far.at[:, part_of], r_far.at[j])
        for o in (2, 1, 3):
            send(far.at[lax.rem(x + o, 4), part_of], q_ref.at[OWN, 1 - h, x, part_of], r_qb.at[x, j], beside(o))
        place(far.at[x, part_of], q_ref.at[OWN, 1 - h, x, part_of], 2 + j)

    def fan_arrived(j):
        for o in (1, 2, 3):
            peer = lax.rem(x + o, 4)
            arrived(q_ref.at[OWN, 1 - h, peer, pl.ds(*CUTS[j])], r_qb.at[peer, j])
        arrived(q_ref.at[OWN, 1 - h, x, pl.ds(*CUTS[j])], local_sem.at[2 + j])

    for o in (1, 2, 3):
        peer = lax.rem(x + o, 4)
        arrived(q_ref.at[OWN, h, peer], r_qa.at[peer])
    mine_a.wait()
    spread(0)
    fan(0)
    fan(1)
    @pl.when(edge)
    def _():
        leave(2).wait_recv()
        leave(3).start()

    fan_arrived(0)
    spread(1)
    fan(2)
    for o in (2, 1, 3):
        send(far.at[pl.ds(2 * h, 2)], own.at[1 - h, x], r_ob.at[x], beside(o))
    own_b = place(far.at[pl.ds(2 * h, 2)], own.at[1 - h, x], 2 + PARTS)
    for o in (2, 1, 3):
        send(far.at[late], extra.at[1 - h, x], r_ex.at[1 - h, x], beside(o))
    extra_b = place(far.at[late], extra.at[1 - h, x], 4 + PARTS)
    fan_arrived(1)
    spread(2)
    fan_arrived(2)
    spread(3)
    relay(1)
    relay(0)
    relay(2)
    relay(3)
    for d in (1, 2, 3):
        arrived(lab_in.at[d - 1], r_lab.at[d - 1])
        row = lab_in[d - 1, d - 1 : d, pl.ds(pl.multiple_of(x * 256, 256), 256)]
        lab_cols[d - 1] = jnp.broadcast_to(row, (8, 256))
    own_a.wait()
    own_b.wait()
    extra_a.wait()
    extra_b.wait()
    for o in (1, 2, 3):
        peer = lax.rem(x + o, 4)
        arrived(own.at[h, peer], r_own.at[peer])
        arrived(own.at[1 - h, peer], r_ob.at[peer])
        for half in range(2):
            arrived(extra.at[half, peer], r_ex.at[half, peer])

    def wide(ref, *at):
        return jnp.concatenate(
            [ref[(*at, half, k)].reshape(-1, 128) for half in range(2) for k in range(4)], axis=1
        )

    def pair(slot):
        scores = lax.dot_general(
            jnp.concatenate([wide(own), wide(extra)], axis=0), wide(q_ref, slot), (((1,), (1,)), ((), ())), preferred_element_type=jnp.float32
        )
        below = slot < OWN
        rows = lab_rows[jnp.where(below, OWN - 1 - slot, ROUNDS)]
        cols = lab_cols[jnp.where(below, ROUNDS, slot - OWN - 1)][:1]
        hit = jnp.concatenate([rows, rows], axis=1) == cols
        base = jnp.where(hit, -0.125, 0.125)
        slope[slot] = (0.125 * jnp.tanh(scores - 0.5) + base).astype(jnp.bfloat16)

    def slot_arrived(slot, delta, indices=range(PARTS + 1)):
        for index in indices:
            arrived(piece(slot, half_of(delta), index), r_z.at[slot, index])

    def step(i, _):
        slot = jnp.where(i == 0, 4 - 2 * c, 0)
        slot = jnp.where(i == 1, 1, slot)
        slot = jnp.where(i == 2, 5, slot)
        slot = jnp.where(i == 3, 2 - 2 * c, slot)
        slot = jnp.where(i == 4, 6 - 2 * c, slot)
        slot = jnp.where(i == 5, 6 * c, slot)

        @pl.when((i == 0) | (i > 2))
        def _():
            slot_arrived(slot, slot - OWN)

        pair(slot)
        return 0

    lax.fori_loop(0, 6, step, 0)

    def store(o, t, k, tile):
        if o == 0 or (o != 2 and t == 3):
            part[o, t, k] = tile
        else:
            small[o - 1, k, t] = tile.astype(jnp.bfloat16)

    def product(k, steps):
        rows, half = (384, 1 - h) if k else (640, h)
        left = jnp.concatenate([slope[s, :rows] for s in SLOTS], axis=1)
        right = jnp.concatenate(
            [
                jnp.concatenate([q_ref[s, half, lax.rem(x + o, 4)].reshape(256, 128) for o in steps], axis=1)
                for s in SLOTS
            ],
            axis=0,
        )
        value = jnp.dot(left, right, preferred_element_type=jnp.float32)
        for at, o in enumerate(steps):
            for group in range(rows // 128):
                tile = value[group * 128 : group * 128 + 128, at * 128 : at * 128 + 128]
                store(o, min(group, 3), k if group < 3 else group - 3, tile)

    def parcel(o, m):
        if m < LAST:
            k, first, end = PARCELS[m]
            at = (o - 1, k, pl.ds(first, end - first))
            return small.at[at], got_small.at[at], r_small.at[o - 1, m]
        if o == 2:
            return small.at[1, :, 3], got_small.at[1, :, 3], r_small.at[1, LAST]
        return part.at[o, 3], got.at[o // 2], r_small.at[o - 1, LAST]

    def give(o, m):
        send(*parcel(o, m), beside(o))

    def take(m):
        for o in (1, 2, 3):
            _, dst, recv = parcel(o, m)
            arrived(dst, recv)

    def total(t, k):
        value = part[0, t, k] + got_small[1, k, t].astype(jnp.float32)
        if t == 3:
            return value + got[0, k] + got[1, k]
        return value + got_small[0, k, t].astype(jnp.float32) + got_small[2, k, t].astype(jnp.float32)

    def finish(m):
        take(m)
        if m == LAST:
            out_ref[h, 3] = total(3, 0)
            out_ref[1 - h, 3] = total(3, 1)
            return
        k, first, end = PARCELS[m]
        for t in range(first, end):
            if k == 1:
                part[0, t, 1] = total(t, 1)
            else:
                out_ref[h, t] = total(t, 0)
        if k == 1:
            rows = pl.ds(first, end - first)
            send(part.at[0, rows, 1], out_ref.at[h, rows], r_out.at[m], across)

    product(1, (2, 1))
    give(2, 0)
    give(1, 0)
    product(1, (3, 0))
    give(3, 0)
    for m in (1, 2):
        for o in (2, 1, 3):
            give(o, m)
    product(0, (2, 1))
    product(0, (3, 0))
    for m in range(3, LAST + 1):
        for o in (2, 1, 3):
            give(o, m)
    for m in range(LAST + 1):
        finish(m)
    for m in range(LAST):
        k, first, end = PARCELS[m]
        if k == 1:
            arrived(out_ref.at[1 - h, pl.ds(first, end - first)], r_out.at[m])
    for copy in sent:
        copy.wait_send()
    for copy, inside in (leave(0), z != 7), (leave(1), z != 0), (leave(2), edge), (leave(3), edge):
        pl.when(inside)(copy.wait_send)


def shards(embeddings, labels):
    bf16, f32, dma = jnp.bfloat16, jnp.float32, pltpu.SemaphoreType.DMA
    block = (4, STRIPES, ROWS, 128)
    out = pl.pallas_call(
        kernel,
        out_shape=jax.ShapeDtypeStruct((2, 4, 128, 128), f32),
        in_specs=[pl.BlockSpec(memory_space=pl.ANY)] * 2,
        out_specs=pl.BlockSpec(memory_space=pltpu.VMEM),
        scratch_shapes=[
            pltpu.VMEM(block, bf16),
            pltpu.VMEM(labels.shape, jnp.int32),
            pltpu.VMEM(block, bf16),
            pltpu.VMEM(block, bf16),
            pltpu.VMEM((7, 2) + block, bf16),
            pltpu.VMEM((2, 4, 2) + block[1:], bf16),
            pltpu.VMEM((2, 4, STRIPES // 2) + block[2:], bf16),
            pltpu.VMEM((7, 640, 256), bf16),
            pltpu.VMEM((ROUNDS + 1, 640, 128), jnp.int32),
            pltpu.VMEM((ROUNDS + 1, 8, 256), jnp.int32),
            pltpu.VMEM((ROUNDS,) + labels.shape, jnp.int32),
            pltpu.VMEM((4, 4, 2, 128, 128), f32),
            pltpu.VMEM((3, 2, 4, 128, 128), bf16),
            pltpu.VMEM((2, 2, 128, 128), f32),
            pltpu.VMEM((3, 2, 4, 128, 128), bf16),
            dma((128,)), dma((5 + PARTS,)), dma((PARTS,)), dma((4,)), dma((4, PARTS)), dma((4,)),
            dma((4,)), dma((2, 4)), dma((7, PARTS + 1)), dma((1,)), dma((3,)), dma((3, 6)), dma((4,)),
        ],
        compiler_params=pltpu.CompilerParams(
            collective_id=0, has_side_effects=True, vmem_limit_bytes=40 * 2**20
        ),
    )(embeddings.reshape(block), labels)
    return out.reshape(1024, 128)


def solution(mesh):
    return jax.shard_map(
        shards,
        mesh=mesh,
        in_specs=(P("play", "col"), P(None, "play")),
        out_specs=P("play", "col"),
        check_vma=False,
    )
```
